32 devices in a mesh: tm: 8 (over z, x), height: 2 (over core), heads: 2 (over y).
Axes of the slice: x: 2, y: 2, z: 4, core: 2. Of those that a mesh axis runs over, the one named last changes fastest.
Arguments:
- queries: bfloat16 [8192, 3072], P(('tm', 'height'), 'heads'), may hold values from -50 to 50
- keys: bfloat16 [8192, 3072], P(('tm', 'height'), 'heads'), may hold values from -12 to 12
- values: bfloat16 [8192, 3072], P(('tm', 'height'), 'heads'), may hold values from -24 to 24
- residual: bfloat16 [8192, 3072], P(('tm', 'height'), 'heads'), may hold values from -3 to 3
- gate: float32 [3072], P('heads'), may hold values from -4 to 4
- out_weight: bfloat16 [3072, 3072], P('heads'), may hold values from -0.109375 to 0.109375
- far_list: int32 [16, 4], replicated, may hold values from 0 to 63, as said below
- far_count: int32 [16], replicated, may hold values from 0 to 4
Outputs:
- mixed: bfloat16 [8192, 3072], P(('tm', 'height'), 'heads')
The draws below stay inside these ranges and needn't reach their ends.
Inputs may be any that keep to these rules, and one draw needn't show every extreme that they name: `far_list`: entries s < far_count[t] of row t name distinct blocks (tile * 4 + block within the tile) of tiles with the same row index as tile t and a frame index that differs from t's by 2 or more, at most one block of any tile; all lists that name a block of a tile u name the same block of u; entries s >= far_count[t] are 0.
All inputs are finite; a program needn't handle non-finite values.
Results may differ from the reference program's by a relative error of at most 0.011.
Values may be sent and summed in bfloat16 or wider, within the bound.
A program may use at most 256 MiB of HBM per device.

```python
import math
import jax
import jax.numpy as jnp
from jax import lax

D = 3072
HEADS = 24
HD = 128
TILE = 512
BLOCK = 128
FAR = 4
TILES = 16
TOKENS = 8192
N_TM = 8
N_HEIGHT = 2
N_HEADS = 2


def radial_lists(key):
    tile_ids = jnp.arange(TILES)
    frame_pos = tile_ids // N_HEIGHT
    row_pos = tile_ids % N_HEIGHT
    centre = jax.random.randint(jax.random.fold_in(key, 1), (), 0, N_TM)
    distance = jnp.abs(frame_pos - centre)
    jitter = jax.random.randint(jax.random.fold_in(key, 2), (TILES,), 0, 3)
    counts = jnp.where(distance == 0, FAR, jnp.maximum(FAR - jitter - distance // 8, 0))
    farthest = jnp.max(distance)
    counts = jnp.where((distance == farthest) & (row_pos == 0), 0, counts)
    usable = (jnp.abs(frame_pos[:, None] - frame_pos[None, :]) >= 2) & (row_pos[:, None] == row_pos[None, :])
    noise_rank = jax.random.randint(jax.random.fold_in(key, 3), (TILES, TILES), 0, 1 << 20)
    ranking = jnp.where(usable, noise_rank * TILES + tile_ids[None, :], 1 << 30)
    picked = jnp.argsort(ranking, axis=1)[:, :FAR]
    offered = jax.random.randint(jax.random.fold_in(key, 4), (TILES,), 0, TILE // BLOCK)
    within = jnp.take(offered, picked)
    listed_ok = jnp.arange(FAR)[None, :] < counts[:, None]
    blocks = jnp.where(listed_ok, picked * (TILE // BLOCK) + within, 0)
    return (blocks.astype(jnp.int32), counts.astype(jnp.int32))


def draw_far_list(key, part):
    blocks, counts = radial_lists(key)
    return blocks


def draw_far_count(key, part):
    blocks, counts = radial_lists(key)
    return counts


def draw_queries(key, part):
    key = jax.random.fold_in(key, 41)
    normal_draw = jax.random.normal(key, (TOKENS, HEADS * HD), jnp.float32)
    result = jnp.clip(math.sqrt(2.0) * normal_draw, -11.0, 11.0)
    return result.astype(jnp.bfloat16)


def draw_keys(key, part):
    key = jax.random.fold_in(key, 43)
    normal_draw = jax.random.normal(key, (TOKENS, HEADS * HD), jnp.float32)
    result = jnp.clip(math.sqrt(2.0) * normal_draw, -11.0, 11.0)
    return result.astype(jnp.bfloat16)


def steps_of(key, extent, split, least, high):
    gain, own = 1.0, jax.random.fold_in(key, 6)
    for dim, shards_of in split:
        draws = jnp.exp(jax.random.uniform(jax.random.fold_in(own, dim), (shards_of,), jnp.float32, least / len(split), high / len(split)))
        gain = gain * jnp.repeat(draws, extent[dim] // shards_of).reshape([-1 if axis == dim else 1 for axis in range(len(extent))])
    return gain


def centred(own_key, extent, scale, bound, pieces=(), kind=jnp.bfloat16):
    entries = jax.random.normal(own_key, extent, jnp.float32) * scale
    if len(pieces) > 0:
        entries = steps_of(own_key, extent, pieces, -0.22, 0.18) * entries
    return jnp.clip(entries, min=-bound, max=bound).astype(kind)


def setup_inputs(seed: int = 0) -> dict:
    seeds = jax.random.split(jax.random.key(seed), 9)
    queries = draw_queries(jax.random.fold_in(seeds[8], 71), 0)
    keys = draw_keys(jax.random.fold_in(seeds[8], 71), 0)
    values = centred(seeds[2], (TOKENS, HEADS * HD), 4.0, 24.0, ((0, 16), (1, 2)))
    residual = centred(seeds[3], (TOKENS, D), 0.5, 3.0, ((0, 16), (1, 2)))
    gate = centred(seeds[4], (D,), 1.0, 4.0, ((0, 2),), jnp.float32)
    out_weight = centred(seeds[5], (HEADS * HD, D), (HEADS * HD) ** -0.5, 0.109375, ((0, 2),))
    far_list = draw_far_list(jax.random.fold_in(seeds[8], 71), 0)
    far_count = draw_far_count(jax.random.fold_in(seeds[8], 71), 0)
    return dict(queries=queries, keys=keys, values=values, residual=residual, gate=gate, out_weight=out_weight, far_list=far_list, far_count=far_count)


def reference(queries, keys, values, residual, gate, out_weight, far_list, far_count):
    width = HEADS * HD
    per_tile = TILE // BLOCK
    scale = 1.0 / math.sqrt(HD)
    key_vals = jnp.concatenate([keys, values], axis=1)
    tile_kv = key_vals.reshape(TILES, TILE, 2 * width)
    block_kv = key_vals.reshape(TILES * per_tile, BLOCK, 2 * width)
    query_tiles = queries.reshape(TILES, TILE, HEADS, HD)

    def one_tile(tile_id):
        frame_pos = tile_id // N_HEIGHT
        row_pos = tile_id % N_HEIGHT
        near_ids = jnp.stack([tile_id, tile_id - N_HEIGHT, tile_id + N_HEIGHT, tile_id - 1, tile_id + 1]).astype(jnp.int32)
        near_ok = jnp.stack([tile_id >= 0, frame_pos > 0, frame_pos < N_TM - 1, row_pos > 0, row_pos < N_HEIGHT - 1])
        near_kv = jnp.take(tile_kv, jnp.clip(near_ids, 0, TILES - 1), axis=0).reshape(5 * TILE, 2 * width)
        listed = far_list[tile_id]
        listed_ok = jnp.arange(FAR) < far_count[tile_id]
        far_kv = jnp.take(block_kv, listed, axis=0).reshape(FAR * BLOCK, 2 * width)
        all_kv = jnp.concatenate([near_kv, far_kv], axis=0)
        key_ok = jnp.concatenate([jnp.repeat(near_ok, TILE), jnp.repeat(listed_ok, BLOCK)])
        key_heads = all_kv[:, :width].reshape(-1, HEADS, HD).astype(jnp.float32)
        value_heads = all_kv[:, width:].reshape(-1, HEADS, HD).astype(jnp.float32)
        query_heads = query_tiles[tile_id].astype(jnp.float32)
        scores = jnp.einsum('qhd,khd->qhk', query_heads, key_heads) * scale
        scores = jnp.where(key_ok[None, None, :], scores, jnp.float32(-1e+30))
        largest = lax.optimization_barrier(jnp.max(scores, axis=-1, keepdims=True))
        weights = jnp.exp(scores - largest)
        total = lax.optimization_barrier(jnp.sum(weights, axis=-1))
        probs = lax.optimization_barrier(weights.astype(jnp.bfloat16)).astype(jnp.float32)
        summed = jnp.einsum('qhk,khd->qhd', probs, value_heads)
        return (summed / total[..., None]).reshape(TILE, width).astype(jnp.bfloat16)
    attended = lax.map(one_tile, jnp.arange(TILES, dtype=jnp.int32)).reshape(TOKENS, width)
    group_cols = HEADS // N_HEADS * HD
    projected = jnp.zeros((TOKENS, D), jnp.float32)
    for group in range(N_HEADS):
        partial_g = jnp.dot(attended[:, group * group_cols:(group + 1) * group_cols], out_weight[group * group_cols:(group + 1) * group_cols], preferred_element_type=jnp.float32)
        projected = projected + lax.optimization_barrier(partial_g.astype(jnp.bfloat16)).astype(jnp.float32)
    return (residual.astype(jnp.float32) + gate[None, :] * projected).astype(jnp.bfloat16)
```

```python
import functools
import math

import jax
import jax.numpy as jnp
from jax import lax
from jax.experimental import pallas as pl
from jax.experimental.pallas import tpu as pltpu
from jax.sharding import PartitionSpec as P

HD = 128
BLOCK = 128
GROUPS = 3
Q_ROWS = 256
EXP2_SCALE = math.log2(math.e) / math.sqrt(HD)


def with_halo(array, sides, width):
    for axis, dim in sides:
        peers, length = (lax.axis_size(axis), array.shape[dim])
        up = [(i, (i + 1) % peers) for i in range(peers - 1)]
        down = [(j, i) for i, j in up]
        last = lax.slice_in_dim(array, length - width, length, axis=dim)
        first = lax.slice_in_dim(array, 0, width, axis=dim)
        before = lax.ppermute(last, axis, up)
        after = lax.ppermute(first, axis, down)
        array = jnp.concatenate([before, array, after], axis=dim)
    return array


def plain_local(queries, keys, values, residual, gate, out_weight, far_list, far_count):
    tile_rows, width_here = queries.shape
    heads_here = width_here // HD
    scale = 1.0 / math.sqrt(HD)
    n_frames = lax.axis_size("tm")
    n_rows = lax.axis_size("height")
    frame_pos = lax.axis_index("tm")
    row_pos = lax.axis_index("height")
    tile_here = frame_pos * n_rows + row_pos
    per_tile = tile_rows // BLOCK
    key_vals = jnp.concatenate([keys, values], axis=1)
    along_frames = with_halo(key_vals[None], (("tm", 0),), 1)
    along_rows = with_halo(key_vals[None], (("height", 0),), 1)
    prior_tile, next_tile = (along_frames[0], along_frames[2])
    below_tile, above_tile = (along_rows[0], along_rows[2])
    listed_ok = jnp.arange(far_list.shape[1])[None, :] < far_count[:, None]
    own_list = lax.dynamic_index_in_dim(far_list, tile_here, 0, False)
    own_ok = lax.dynamic_index_in_dim(listed_ok, tile_here, 0, False)
    own_source = own_list // per_tile // n_rows
    frame_ok = jnp.any(
        own_ok[None, :] & (own_source[None, :] == jnp.arange(n_frames)[:, None]), axis=1
    )
    query_heads = queries.reshape(tile_rows, heads_here, HD)

    def attend(carried, block_kv, key_ok):
        best_so_far, total, weighted = carried
        key_heads = block_kv[:, :width_here].reshape(-1, heads_here, HD)
        value_heads = block_kv[:, width_here:].reshape(-1, heads_here, HD)
        scores = (
            jnp.einsum("qhd,khd->qhk", query_heads, key_heads, preferred_element_type=jnp.float32)
            * scale
        )
        scores = jnp.where(key_ok[None, None, :], scores, jnp.float32(-1e30))
        new_best = jnp.maximum(best_so_far, jnp.max(scores, axis=-1))
        fade = jnp.exp(best_so_far - new_best)
        weights = jnp.exp(scores - new_best[..., None])
        total = total * fade + jnp.sum(weights, axis=-1)
        weighted = weighted * fade[..., None] + jnp.einsum(
            "qhk,khd->qhd",
            weights.astype(jnp.bfloat16),
            value_heads,
            preferred_element_type=jnp.float32,
        )
        return (new_best, total, weighted)

    carried = (
        jnp.full((tile_rows, heads_here), -1e30, jnp.float32),
        jnp.zeros((tile_rows, heads_here), jnp.float32),
        jnp.zeros((tile_rows, heads_here, HD), jnp.float32),
    )
    first_kv = jnp.concatenate([key_vals, prior_tile, next_tile], axis=0)
    first_ok = jnp.repeat(
        jnp.stack([frame_pos >= 0, frame_pos > 0, frame_pos < n_frames - 1]), tile_rows
    )
    carried = attend(carried, first_kv, first_ok)
    second_kv = jnp.concatenate([below_tile, above_tile], axis=0)
    second_ok = jnp.repeat(jnp.stack([row_pos > 0, row_pos < n_rows - 1]), tile_rows)
    carried = attend(carried, second_kv, second_ok)
    blocks_here = key_vals.reshape(per_tile, BLOCK, 2 * width_here)
    band_lists = lax.dynamic_index_in_dim(far_list.reshape(n_frames, n_rows, -1), row_pos, 1, False)
    band_ok = lax.dynamic_index_in_dim(listed_ok.reshape(n_frames, n_rows, -1), row_pos, 1, False)
    requested = band_ok & (band_lists // per_tile == tile_here)
    wanted = jnp.sum(jnp.where(requested, band_lists % per_tile, 0), axis=1)
    outgoing = jnp.take(blocks_here, wanted, axis=0)
    arrived = lax.all_to_all(outgoing, "tm", split_axis=0, concat_axis=0, tiled=True)
    attend_carried = carried
    slot_count = arrived.shape[0]
    group_size = math.gcd(slot_count, 16)
    for offset in range(0, slot_count, group_size):
        segment = arrived[offset : offset + group_size].reshape(group_size * BLOCK, 2 * width_here)
        segment_ok = jnp.repeat(frame_ok[offset : offset + group_size], BLOCK)
        attend_carried = attend(attend_carried, segment, segment_ok)
    carried = attend_carried
    best_so_far, total, weighted = carried
    attended = (weighted / total[..., None]).reshape(tile_rows, width_here).astype(jnp.bfloat16)
    projected = jnp.dot(attended, out_weight, preferred_element_type=jnp.float32)
    summed = lax.psum_scatter(
        projected.astype(jnp.bfloat16), "heads", scatter_dimension=1, tiled=True
    ).astype(jnp.float32)
    return (residual.astype(jnp.float32) + gate[None, :] * summed).astype(jnp.bfloat16)


def attention_kernel(far_entries, info, mine, got, side_mine, side_got, near_mine, near_got, far, out):
    f32 = jnp.float32
    rows = mine.shape[1]
    ones = jnp.ones((rows, HD), jnp.bfloat16)
    far_rows = far_entries * BLOCK
    for p in range(2):
        own, other = ((mine, got), (got, mine))[p]
        side = (side_mine, side_got)[p]
        near = (near_mine, near_got)[p]
        picked = [(info[p, 2 * s], info[p, 2 * s + 1]) for s in range(far_entries)]
        far_k = jnp.concatenate([far[z, j, 0] for z, j in picked], axis=0)
        far_v = jnp.concatenate([far[z, j, 1] for z, j in picked], axis=0)
        count = info[p, 2 * far_entries]
        near_ok = info[p, 2 * far_entries + 1]
        block_of = lax.broadcasted_iota(jnp.int32, (1, far_rows), 1) // BLOCK
        far_bias = jnp.where(block_of < count, f32(0), f32(-1e30))
        near_bias = jnp.where(
            jnp.full((1, rows), near_ok, jnp.int32) > 0, f32(0), f32(-1e30)
        )
        pieces = [
            (own[0], own[1], None),
            (other[0], other[1], None),
            (side[0], side[1], None),
            (near[0], near[1], near_bias),
            (far_k, far_v, far_bias),
        ]
        for q0 in range(0, rows, Q_ROWS):
            q = own[2, q0 : q0 + Q_ROWS]
            scores = []
            for k, _, bias in pieces:
                s = lax.dot_general(q, k, (((1,), (1,)), ((), ())), preferred_element_type=f32)
                scores.append(s if bias is None else s + bias)
            largest = scores[0].max(axis=1, keepdims=True)
            for s in scores[1:]:
                largest = jnp.maximum(largest, s.max(axis=1, keepdims=True))
            total = jnp.zeros((Q_ROWS, 2 * HD), f32)
            for s, (_, v, _) in zip(scores, pieces):
                weights = jnp.exp2((s - largest) * EXP2_SCALE).astype(jnp.bfloat16)
                v_ones = jnp.concatenate([v, ones[: v.shape[0]]], axis=1)
                total = total + jnp.dot(weights, v_ones, preferred_element_type=f32)
            out[p, q0 : q0 + Q_ROWS] = (total[:, :HD] / total[:, HD:]).astype(jnp.bfloat16)


def attention(info, mine, got, side_mine, side_got, near_mine, near_got, far):
    rows, width = mine.shape[1:]
    far_entries = (info.shape[1] - 2) // 2

    def spec(array):
        lead = array.shape[:-1]
        return pl.BlockSpec(lead + (HD,), lambda h: (0,) * len(lead) + (h,))

    arrays = (mine, got, side_mine, side_got, near_mine, near_got, far)
    keys = 4 * rows + far_entries * BLOCK
    return pl.pallas_call(
        functools.partial(attention_kernel, far_entries),
        grid=(width // HD,),
        out_shape=jax.ShapeDtypeStruct((2, rows, width), jnp.bfloat16),
        in_specs=[pl.BlockSpec(memory_space=pltpu.SMEM)] + [spec(a) for a in arrays],
        out_specs=pl.BlockSpec((2, rows, HD), lambda h: (0, 0, h)),
        compiler_params=pltpu.CompilerParams(vmem_limit_bytes=48 * 2**20),
        cost_estimate=pl.CostEstimate(
            flops=2 * rows * keys * width * 8,
            bytes_accessed=sum(a.size * 2 for a in arrays),
            transcendentals=2 * rows * keys * width // HD,
        ),
    )(info, *arrays)


def paired_local(queries, keys, values, residual, gate, out_weight, far_list, far_count):
    rows, width = queries.shape
    half = width // 2
    n_frames, n_rows = lax.axis_size("tm"), lax.axis_size("height")
    frame, row = lax.axis_index("tm"), lax.axis_index("height")
    group_y = lax.axis_index("heads")
    x, z = frame % 2, frame // 2
    n_z = n_frames // 2
    per_tile = rows // BLOCK
    far_entries = far_list.shape[1]
    swap_x = [(i, i ^ 1) for i in range(n_frames)]
    direct = [(2 * i + 1, 2 * i + 3) for i in range(n_z - 1)]
    direct += [(2 * i + 2, 2 * i) for i in range(n_z - 1)]
    onward = [(2 * i, 2 * i + 2) for i in range(n_z - 1)]
    onward += [(2 * i + 3, 2 * i + 1) for i in range(n_z - 1)]
    swap = [(0, 1), (1, 0)]

    listed_ok = jnp.arange(far_entries)[None, :] < far_count[:, None]
    tiles = jnp.arange(n_frames * n_rows)
    named = listed_ok[None] & (far_list[None] // per_tile == tiles[:, None, None])
    offered = jnp.max(jnp.where(named, far_list[None] % per_tile, 0), axis=(1, 2))
    info_rows = []
    for p, f in ((0, frame), (1, frame ^ 1)):
        t = f * n_rows + row
        source = far_list[t] // per_tile // n_rows
        pairs = jnp.stack([source // 2, (source % 2) ^ x], axis=1).reshape(-1)
        parity = x ^ p
        near_ok = jnp.where(parity == 0, z > 0, z < n_z - 1).astype(jnp.int32)
        info_rows.append(jnp.concatenate([pairs, jnp.stack([far_count[t], near_ok])]))
    info = jnp.stack(info_rows).astype(jnp.int32)
    off_mine = offered[frame * n_rows + row] * BLOCK
    off_got = offered[(frame ^ 1) * n_rows + row] * BLOCK

    wide = width // n_rows
    w_theirs = lax.dynamic_slice(out_weight, (row * wide, (1 - group_y) * width), (wide, width))
    w_first = lax.ppermute(w_theirs, "heads", swap)
    w_second = lax.ppermute(w_first, "height", swap)
    w_other = jnp.where(
        row == 0,
        jnp.concatenate([w_first, w_second], axis=0),
        jnp.concatenate([w_second, w_first], axis=0),
    )
    w_own = lax.dynamic_slice(out_weight, (0, group_y * width), (width, width))

    step = half // GROUPS
    projected = None
    for g in range(GROUPS):
        here = x * half + g * step
        there = (1 - x) * half + g * step

        def cut(array, start):
            return lax.dynamic_slice(array, (0, start), (rows, step))

        got_kv = lax.ppermute(jnp.stack([cut(keys, there), cut(values, there)]), "tm", swap_x)
        got_q = lax.ppermute(cut(queries, there), "tm", swap_x)
        mine_kv = jnp.stack([cut(keys, here), cut(values, here)])
        mine = jnp.concatenate([mine_kv, cut(queries, here)[None]])
        got = jnp.concatenate([got_kv, got_q[None]])
        near_got = lax.ppermute(mine_kv, "tm", direct)
        near_mine = lax.ppermute(got_kv, "tm", onward)
        side_mine = lax.ppermute(mine_kv, "height", swap)
        side_got = lax.ppermute(got_kv, "height", swap)
        offer = jnp.stack([
            lax.dynamic_slice(mine_kv, (0, off_mine, 0), (2, BLOCK, step)),
            lax.dynamic_slice(got_kv, (0, off_got, 0), (2, BLOCK, step)),
        ])
        far = lax.all_gather(
            offer, "tm",
            axis_index_groups=[[2 * i + e for i in range(n_z)] for e in range(2)],
        )
        done = attention(info, mine, got, side_mine, side_got, near_mine, near_got, far)
        back = lax.ppermute(done[1], "tm", swap_x)
        both = jnp.concatenate([done[0], back], axis=1)
        across = lax.ppermute(both, "heads", swap)
        w_rows = [
            lax.dynamic_slice(w, (s, 0), (step, width))
            for w in (w_own, w_other) for s in (here, there)
        ]
        part = jnp.dot(both, jnp.concatenate(w_rows[:2]), preferred_element_type=jnp.float32)
        part = part + jnp.dot(across, jnp.concatenate(w_rows[2:]), preferred_element_type=jnp.float32)
        projected = part if projected is None else projected + part
    return (residual.astype(jnp.float32) + gate[None, :] * projected).astype(jnp.bfloat16)


def solution(mesh):
    sizes = dict(mesh.shape)

    def local(queries, *rest):
        width = queries.shape[1]
        paired = sizes["tm"] % 2 == 0 and sizes["height"] == 2 and sizes["heads"] == 2
        if paired and width % (2 * GROUPS * HD) == 0:
            return paired_local(queries, *rest)
        return plain_local(queries, *rest)

    return jax.shard_map(
        local,
        mesh=mesh,
        in_specs=(
            P(("tm", "height"), "heads"),
            P(("tm", "height"), "heads"),
            P(("tm", "height"), "heads"),
            P(("tm", "height"), "heads"),
            P("heads"),
            P("heads", None),
            P(),
            P(),
        ),
        out_specs=P(("tm", "height"), "heads"),
        check_vma=False,
    )
```

```python
import functools
import math

import jax
import jax.numpy as jnp
from jax import lax
from jax.experimental import pallas as pl
from jax.experimental.pallas import tpu as pltpu
from jax.sharding import PartitionSpec as P

HD = 128
BLOCK = 128
Q_ROWS = 256
AHEAD = 2
MESH = pl.DeviceIdType.MESH
EXP2_SCALE = math.log2(math.e) / math.sqrt(HD)


def with_halo(array, sides, width):
    for axis, dim in sides:
        peers, length = (lax.axis_size(axis), array.shape[dim])
        up = [(i, (i + 1) % peers) for i in range(peers - 1)]
        down = [(j, i) for i, j in up]
        last = lax.slice_in_dim(array, length - width, length, axis=dim)
        first = lax.slice_in_dim(array, 0, width, axis=dim)
        before = lax.ppermute(last, axis, up)
        after = lax.ppermute(first, axis, down)
        array = jnp.concatenate([before, array, after], axis=dim)
    return array


def plain_local(queries, keys, values, residual, gate, out_weight, far_list, far_count):
    tile_rows, width_here = queries.shape
    heads_here = width_here // HD
    scale = 1.0 / math.sqrt(HD)
    n_frames = lax.axis_size("tm")
    n_rows = lax.axis_size("height")
    frame_pos = lax.axis_index("tm")
    row_pos = lax.axis_index("height")
    tile_here = frame_pos * n_rows + row_pos
    per_tile = tile_rows // BLOCK
    key_vals = jnp.concatenate([keys, values], axis=1)
    along_frames = with_halo(key_vals[None], (("tm", 0),), 1)
    along_rows = with_halo(key_vals[None], (("height", 0),), 1)
    prior_tile, next_tile = (along_frames[0], along_frames[2])
    below_tile, above_tile = (along_rows[0], along_rows[2])
    listed_ok = jnp.arange(far_list.shape[1])[None, :] < far_count[:, None]
    own_list = lax.dynamic_index_in_dim(far_list, tile_here, 0, False)
    own_ok = lax.dynamic_index_in_dim(listed_ok, tile_here, 0, False)
    own_source = own_list // per_tile // n_rows
    frame_ok = jnp.any(
        own_ok[None, :] & (own_source[None, :] == jnp.arange(n_frames)[:, None]), axis=1
    )
    query_heads = queries.reshape(tile_rows, heads_here, HD)

    def attend(carried, block_kv, key_ok):
        best_so_far, total, weighted = carried
        key_heads = block_kv[:, :width_here].reshape(-1, heads_here, HD)
        value_heads = block_kv[:, width_here:].reshape(-1, heads_here, HD)
        scores = (
            jnp.einsum("qhd,khd->qhk", query_heads, key_heads, preferred_element_type=jnp.float32)
            * scale
        )
        scores = jnp.where(key_ok[None, None, :], scores, jnp.float32(-1e30))
        new_best = jnp.maximum(best_so_far, jnp.max(scores, axis=-1))
        fade = jnp.exp(best_so_far - new_best)
        weights = jnp.exp(scores - new_best[..., None])
        total = total * fade + jnp.sum(weights, axis=-1)
        weighted = weighted * fade[..., None] + jnp.einsum(
            "qhk,khd->qhd",
            weights.astype(jnp.bfloat16),
            value_heads,
            preferred_element_type=jnp.float32,
        )
        return (new_best, total, weighted)

    carried = (
        jnp.full((tile_rows, heads_here), -1e30, jnp.float32),
        jnp.zeros((tile_rows, heads_here), jnp.float32),
        jnp.zeros((tile_rows, heads_here, HD), jnp.float32),
    )
    first_kv = jnp.concatenate([key_vals, prior_tile, next_tile], axis=0)
    first_ok = jnp.repeat(
        jnp.stack([frame_pos >= 0, frame_pos > 0, frame_pos < n_frames - 1]), tile_rows
    )
    carried = attend(carried, first_kv, first_ok)
    second_kv = jnp.concatenate([below_tile, above_tile], axis=0)
    second_ok = jnp.repeat(jnp.stack([row_pos > 0, row_pos < n_rows - 1]), tile_rows)
    carried = attend(carried, second_kv, second_ok)
    blocks_here = key_vals.reshape(per_tile, BLOCK, 2 * width_here)
    band_lists = lax.dynamic_index_in_dim(far_list.reshape(n_frames, n_rows, -1), row_pos, 1, False)
    band_ok = lax.dynamic_index_in_dim(listed_ok.reshape(n_frames, n_rows, -1), row_pos, 1, False)
    requested = band_ok & (band_lists // per_tile == tile_here)
    wanted = jnp.sum(jnp.where(requested, band_lists % per_tile, 0), axis=1)
    outgoing = jnp.take(blocks_here, wanted, axis=0)
    arrived = lax.all_to_all(outgoing, "tm", split_axis=0, concat_axis=0, tiled=True)
    attend_carried = carried
    slot_count = arrived.shape[0]
    group_size = math.gcd(slot_count, 16)
    for offset in range(0, slot_count, group_size):
        segment = arrived[offset : offset + group_size].reshape(group_size * BLOCK, 2 * width_here)
        segment_ok = jnp.repeat(frame_ok[offset : offset + group_size], BLOCK)
        attend_carried = attend(attend_carried, segment, segment_ok)
    carried = attend_carried
    best_so_far, total, weighted = carried
    attended = (weighted / total[..., None]).reshape(tile_rows, width_here).astype(jnp.bfloat16)
    projected = jnp.dot(attended, out_weight, preferred_element_type=jnp.float32)
    summed = lax.psum_scatter(
        projected.astype(jnp.bfloat16), "heads", scatter_dimension=1, tiled=True
    ).astype(jnp.float32)
    return (residual.astype(jnp.float32) + gate[None, :] * summed).astype(jnp.bfloat16)


def attend_rows(q, pieces):
    f32 = jnp.float32
    scores = []
    for k, _, bias in pieces:
        s = lax.dot_general(q, k, (((1,), (1,)), ((), ())), preferred_element_type=f32)
        scores.append(s if bias is None else s + bias)
    largest = scores[0].max(axis=1, keepdims=True)
    for s in scores[1:]:
        largest = jnp.maximum(largest, s.max(axis=1, keepdims=True))
    total = jnp.zeros((q.shape[0], 2 * HD), f32)
    for s, (_, v, _) in zip(scores, pieces):
        weights = jnp.exp2((s - largest) * EXP2_SCALE).astype(jnp.bfloat16)
        v_ones = jnp.concatenate([v, jnp.ones_like(v)], axis=1)
        total = total + jnp.dot(weights, v_ones, preferred_element_type=f32)
    return (total[:, :HD] / total[:, HD:]).astype(jnp.bfloat16)


def paired_kernel(
    n_z, pick, near_bias, far_bias, keys, values, queries, weight, att, w_other,
    got, near_mine, near_got, side_mine, side_got, far, done,
    x_send, x_recv, direct_send, direct_recv, onward_send, onward_recv,
    side_send, side_recv, pass_send, pass_recv, up_send, down_send, far_recv,
    back_send, back_recv, y_send, y_recv, w_send, w_recv,
):
    frame, row, group_y = lax.axis_index("tm"), lax.axis_index("height"), lax.axis_index("heads")
    x, z = frame % 2, frame // 2
    rows, width = keys.shape
    half = width // 2
    n_heads = half // HD
    per_tile = rows // BLOCK
    above, below = z < n_z - 1, z > 0
    partner = frame + 1 - 2 * x
    direct_to = jnp.where(x == 1, frame + 2, frame - 2)
    onward_to = jnp.where(x == 1, frame - 2, frame + 2)
    direct_out = (x == 1) & above | (x == 0) & below
    direct_in = (x == 1) & below | (x == 0) & above

    def cols(start, h):
        return pl.ds(pl.multiple_of(start + h * HD, HD), HD)

    def mine_cols(h):
        return cols(x * half, h)

    def remote(src, dst, send, recv, to):
        return pltpu.make_async_remote_copy(
            src_ref=src, dst_ref=dst, send_sem=send, recv_sem=recv,
            device_id=to, device_id_type=MESH,
        )

    def x_copy(h, a):
        src = (keys, values, queries)[a].at[:, cols((1 - x) * half, h)]
        return remote(src, got.at[h, a], x_send.at[h, a], x_recv.at[h, a], {"tm": partner})

    def direct_copy(h, a):
        src = (keys, values)[a].at[:, mine_cols(h)]
        return remote(src, near_got.at[h, a], direct_send.at[h, a], direct_recv.at[h, a], {"tm": direct_to})

    def side_copy(h, a):
        src = (keys, values)[a].at[:, mine_cols(h)]
        return remote(src, side_mine.at[h, a], side_send.at[h, a], side_recv.at[h, a], {"height": 1 - row})

    def onward_copy(h):
        return remote(got.at[h, pl.ds(0, 2)], near_mine.at[h], onward_send.at[h], onward_recv.at[h], {"tm": onward_to})

    def pass_copy(h):
        return remote(got.at[h, pl.ds(0, 2)], side_got.at[h], pass_send.at[h], pass_recv.at[h], {"height": 1 - row})

    def up_copy(h, o):
        return remote(far.at[h, o], far.at[h, o], up_send.at[h, o], far_recv.at[h, o], {"tm": frame + 2})

    def down_copy(h, o):
        return remote(far.at[h, o], far.at[h, o], down_send.at[h, o], far_recv.at[h, o], {"tm": frame - 2})

    def back_copy(h):
        return remote(done.at[h], att.at[:, mine_cols(h)], back_send.at[h], back_recv.at[h], {"tm": partner})

    def y_copy(h, a):
        start = x * half if a == 0 else (1 - x) * half
        src = att.at[:, cols(start, h)]
        dst = att.at[:, cols(width + start, h)]
        return remote(src, dst, y_send.at[h, a], y_recv.at[h, a], {"heads": 1 - group_y})

    wide = width // 2

    def w_copy():
        src = weight.at[pl.ds(row * wide, wide), pl.ds(pl.multiple_of((1 - group_y) * width, width), width)]
        return remote(src, w_other.at[pl.ds(row * wide, wide)], w_send.at[0], w_recv.at[0], {"heads": 1 - group_y})

    def w_pass():
        part = w_other.at[pl.ds(row * wide, wide)]
        return remote(part, part, w_send.at[1], w_recv.at[1], {"height": 1 - row})

    barrier = pltpu.get_barrier_semaphore()
    for to in ({"tm": partner}, {"height": 1 - row}, {"heads": 1 - group_y}):
        pl.semaphore_signal(barrier, inc=1, device_id=to, device_id_type=MESH)

    @pl.when(above)
    def _():
        pl.semaphore_signal(barrier, inc=1, device_id={"tm": frame + 2}, device_id_type=MESH)

    @pl.when(below)
    def _():
        pl.semaphore_signal(barrier, inc=1, device_id={"tm": frame - 2}, device_id_type=MESH)

    pl.semaphore_wait(barrier, 3 + above.astype(jnp.int32) + below.astype(jnp.int32))

    def start_head(h):
        for a in range(2):
            x_copy(h, a).start()
            side_copy(h, a).start()

        @pl.when(direct_out)
        def _():
            for a in range(2):
                direct_copy(h, a).start()

        x_copy(h, 2).start()

    lax.fori_loop(0, AHEAD, lambda h, c: (start_head(h), c)[1], 0)
    w_copy().start()

    @pl.when(jnp.logical_not(direct_in))
    def _():
        near_got[...] = jnp.zeros_like(near_got)

    @pl.when(jnp.logical_not(direct_out))
    def _():
        near_mine[...] = jnp.zeros_like(near_mine)

    def offered(block, p):
        total = jnp.zeros((BLOCK, HD), jnp.float32)
        for b in range(per_tile):
            total = total + block(b).astype(jnp.float32) * pick[p, b]
        return total.astype(jnp.bfloat16)

    def arrive(h):
        for a in range(2):
            x_copy(h, a).wait_recv()

        @pl.when(direct_in)
        def _():
            onward_copy(h).start()

        pass_copy(h).start()
        for a, own in enumerate((keys, values)):
            far[h, z, 0, a] = offered(lambda b: own[b * BLOCK : (b + 1) * BLOCK, mine_cols(h)], 0)
            far[h, z, 1, a] = offered(lambda b: got[h, a, b * BLOCK : (b + 1) * BLOCK], 1)

        @pl.when(above)
        def _():
            up_copy(h, z).start()

        @pl.when(below)
        def _():
            down_copy(h, z).start()

    def hop(h, k):
        @pl.when(z >= k)
        def _():
            up_copy(h, z - k).wait_recv()

            @pl.when(above)
            def _():
                up_copy(h, z - k).start()

        @pl.when(z + k < n_z)
        def _():
            down_copy(h, z + k).wait_recv()

            @pl.when(below)
            def _():
                down_copy(h, z + k).start()

    def compute(h):
        x_copy(h, 2).wait_recv()
        for a in range(2):
            side_copy(h, a).wait_recv()
        pass_copy(h).wait_recv()

        @pl.when(direct_in)
        def _():
            for a in range(2):
                direct_copy(h, a).wait_recv()

        @pl.when(direct_out)
        def _():
            onward_copy(h).wait_recv()

        k_mine, v_mine = keys[:, mine_cols(h)], values[:, mine_cols(h)]
        far_k = far[h, :, :, 0].reshape(n_z * 2 * BLOCK, HD)
        far_v = far[h, :, :, 1].reshape(n_z * 2 * BLOCK, HD)
        pair = [(k_mine, v_mine, None), (got[h, 0], got[h, 1], None)]
        theirs = pair + [
            (side_got[h, 0], side_got[h, 1], None),
            (near_got[h, 0], near_got[h, 1], near_bias[1:2]),
            (far_k, far_v, far_bias[1:2]),
        ]
        for q0 in range(0, rows, Q_ROWS):
            done[h, q0 : q0 + Q_ROWS] = attend_rows(got[h, 2, q0 : q0 + Q_ROWS], theirs)
        back_copy(h).start()
        ours = pair + [
            (side_mine[h, 0], side_mine[h, 1], None),
            (near_mine[h, 0], near_mine[h, 1], near_bias[0:1]),
            (far_k, far_v, far_bias[0:1]),
        ]
        for q0 in range(0, rows, Q_ROWS):
            att[q0 : q0 + Q_ROWS, mine_cols(h)] = attend_rows(
                queries[q0 : q0 + Q_ROWS, mine_cols(h)], ours
            )
        y_copy(h, 0).start()

    def across(h):
        remote(
            done.at[h], att.at[:, cols((1 - x) * half, h)], back_send.at[h], back_recv.at[h], {"tm": partner}
        ).wait_recv()
        y_copy(h, 1).start()

    def stage(i, lag, work):
        @pl.when((i >= lag) & (i - lag < n_heads))
        def _():
            work(i - lag)

    def step(i, carry):
        @pl.when(i + AHEAD < n_heads)
        def _():
            start_head(i + AHEAD)

        stage(i, 0, arrive)
        for k in range(1, n_z):
            stage(i, k, lambda h, k=k: hop(h, k))
        stage(i, n_z - 1, compute)
        stage(i, n_z, across)

        @pl.when(i == n_heads)
        def _():
            w_copy().wait_recv()
            w_pass().start()

        return carry

    lax.fori_loop(0, n_heads + n_z, step, 0)

    def finish(h, carry):
        for a in range(3):
            x_copy(h, a).wait_send()
        for a in range(2):
            side_copy(h, a).wait_send()
            y_copy(h, a).wait_send()
            y_copy(h, a).wait_recv()
        pass_copy(h).wait_send()
        back_copy(h).wait_send()

        @pl.when(direct_out)
        def _():
            for a in range(2):
                direct_copy(h, a).wait_send()

        @pl.when(direct_in)
        def _():
            onward_copy(h).wait_send()

        for o in range(n_z):
            @pl.when(above & (z >= o))
            def _():
                up_copy(h, o).wait_send()

            @pl.when(below & (z <= o))
            def _():
                down_copy(h, o).wait_send()

        return carry

    lax.fori_loop(0, n_heads, finish, 0)
    w_copy().wait_send()
    w_pass().wait_send()
    other = w_other.at[pl.ds((1 - row) * wide, wide)]
    remote(other, other, w_send.at[1], w_recv.at[1], {"height": 1 - row}).wait_recv()


def paired_local(queries, keys, values, residual, gate, out_weight, far_list, far_count):
    rows, width = queries.shape
    n_frames, n_rows = lax.axis_size("tm"), lax.axis_size("height")
    frame, row = lax.axis_index("tm"), lax.axis_index("height")
    group_y = lax.axis_index("heads")
    x, z = frame % 2, frame // 2
    n_z = n_frames // 2
    n_heads = width // 2 // HD
    per_tile = rows // BLOCK
    far_entries = far_list.shape[1]
    f32 = jnp.float32

    listed_ok = jnp.arange(far_entries)[None, :] < far_count[:, None]
    own_tiles = jnp.stack([frame, frame ^ 1]) * n_rows + row
    named = listed_ok[None] & (far_list[None] // per_tile == own_tiles[:, None, None])
    offered = jnp.max(jnp.where(named, far_list[None] % per_tile, 0), axis=(1, 2))
    pick = (offered[:, None] == jnp.arange(per_tile)[None, :]).astype(f32)
    source = far_list[own_tiles] // per_tile // n_rows
    slot_frames = jnp.arange(n_frames) ^ x
    live = (source[:, :, None] == slot_frames[None, None, :]) & listed_ok[own_tiles][:, :, None]
    far_bias = jnp.repeat(jnp.where(jnp.any(live, axis=1), f32(0), f32(-1e30)), BLOCK, axis=1)
    near_ok = jnp.where(jnp.stack([x, x ^ 1]) == 0, z > 0, z < n_z - 1)
    near_bias = jnp.broadcast_to(jnp.where(near_ok, f32(0), f32(-1e30))[:, None], (2, rows))

    bf16 = jnp.bfloat16
    vmem, dma = pltpu.VMEM, pltpu.SemaphoreType.DMA
    any_spec, vmem_spec = pl.BlockSpec(memory_space=pl.ANY), pl.BlockSpec(memory_space=pltpu.VMEM)
    pair_buffer = vmem((n_heads, 2, rows, HD), bf16)
    keys_seen = 4 * rows + n_frames * BLOCK
    att, w_other = pl.pallas_call(
        functools.partial(paired_kernel, n_z),
        out_shape=[
            jax.ShapeDtypeStruct((rows, 2 * width), bf16),
            jax.ShapeDtypeStruct((width, width), bf16),
        ],
        in_specs=[pl.BlockSpec(memory_space=pltpu.SMEM)] + [vmem_spec] * 5 + [any_spec],
        out_specs=[vmem_spec, any_spec],
        scratch_shapes=[vmem((n_heads, 3, rows, HD), bf16)]
        + [pair_buffer] * 4
        + [vmem((n_heads, n_z, 2, 2, BLOCK, HD), bf16), vmem((n_heads, rows, HD), bf16)]
        + [dma((n_heads, 3))] * 2
        + [dma((n_heads, 2))] * 2
        + [dma((n_heads,))] * 2
        + [dma((n_heads, 2))] * 2
        + [dma((n_heads,))] * 2
        + [dma((n_heads, n_z))] * 3
        + [dma((n_heads,))] * 2
        + [dma((n_heads, 2))] * 2
        + [dma((2,))] * 2,
        compiler_params=pltpu.CompilerParams(
            collective_id=0, has_side_effects=True, vmem_limit_bytes=56 * 2**20
        ),
        cost_estimate=pl.CostEstimate(
            flops=8 * rows * keys_seen * width, bytes_accessed=30 * rows * width,
            transcendentals=rows * keys_seen * width // HD,
        ),
    )(pick, near_bias, far_bias, keys, values, queries, out_weight)
    w_own = lax.dynamic_slice(out_weight, (0, group_y * width), (width, width))
    projected = jnp.dot(att[:, :width], w_own, preferred_element_type=f32)
    projected = projected + jnp.dot(att[:, width:], w_other, preferred_element_type=f32)
    return (residual.astype(f32) + gate[None, :] * projected).astype(bf16)


def solution(mesh):
    sizes = dict(mesh.shape)

    def local(queries, *rest):
        width = queries.shape[1]
        paired = sizes["tm"] % 2 == 0 and sizes["height"] == 2 and sizes["heads"] == 2
        if paired and width % (2 * HD) == 0:
            return paired_local(queries, *rest)
        return plain_local(queries, *rest)

    return jax.shard_map(
        local,
        mesh=mesh,
        in_specs=(
            P(("tm", "height"), "heads"),
            P(("tm", "height"), "heads"),
            P(("tm", "height"), "heads"),
            P(("tm", "height"), "heads"),
            P("heads"),
            P("heads", None),
            P(),
            P(),
        ),
        out_specs=P(("tm", "height"), "heads"),
        check_vma=False,
    )
```
